512 devices in a mesh: dp: 32 (over x, z_lo), group: 8 (over z_hi, y), half: 2 (over core).
Axes of the slice: x: 4, y: 4, z: 16 (z_hi: 2, z_lo: 8; z = z_hi * 8 + z_lo), core: 2. Of those that a mesh axis runs over, the one named last changes fastest.
Arguments:
- activations: bfloat16 [8192, 8192], P('dp', ('group', 'half')), may hold values from -6 to 6
- output_grads: bfloat16 [8192, 28672], P('dp', ('group', 'half')), may hold values from -6 to 6
- out_factors: bfloat16 [1024, 28672], P('dp', ('group', 'half')), may hold values from -0.005859375 to 0.005859375
- in_factors: bfloat16 [1024, 8192], P('dp', ('group', 'half')), may hold values from -0.0625 to 0.0625
- basis: bfloat16 [8192, 8192], P(('group', 'half'), 'dp'), may hold values from -0.0625 to 0.0625
- eigvals: float32 [8192], P('dp'), may hold values from 0.1 to 10
Outputs:
- influence: float32 [8192, 32], P(('dp', 'group', 'half'))
The draws below stay inside these ranges and needn't reach their ends.
All inputs are finite; a program needn't handle non-finite values.
Results may differ from the reference program's by a relative error of at most 0.0038.
Values may be sent and summed in bfloat16 or wider, within the bound.
No kernel may reach another device: no remote copies, remote signals or barrier semaphores. Data moves between devices by JAX's collectives and lax.ppermute only.
A program may use at most 64 MiB of HBM per device.

```python
import math
import jax
import jax.numpy as jnp
from jax import lax

D = 8192
FF = 28672
RANK = 32
TOK_DEV = 256
QUERIES = 32
TOKENS = 8192
N_DP = 32


def level_of(stream_key, dims, pieces, least, high):
    def one(axis_at, blocks):
        draws = jax.random.uniform(jax.random.fold_in(jax.random.fold_in(stream_key, 6), axis_at), (blocks,), jnp.float32, least / len(pieces), high / len(pieces))
        return jnp.repeat(jnp.exp(draws), dims[axis_at] // blocks).reshape((-1,) + (1,) * (len(dims) - axis_at - 1))

    level = one(*pieces[0])
    for cut in pieces[1:]:
        level = level * one(*cut)
    return level


def bell_draw(stream_key, shape, spread, limit, cuts=(), held_as=jnp.bfloat16):
    factor_of = level_of(stream_key, shape, cuts, -0.22, 0.18) if cuts else 1.0
    drawn = jax.random.normal(stream_key, shape, jnp.float32) * spread * factor_of
    return jnp.minimum(jnp.maximum(drawn, -limit), limit).astype(held_as)


def setup_inputs(seed: int = 0) -> dict:
    arg_keys = jax.random.split(jax.random.key(seed), 7)
    return {
        "activations": bell_draw(arg_keys[0], (TOKENS, D), 1.0, 6.0, ((0, 32), (1, 16))),
        "output_grads": bell_draw(arg_keys[1], (TOKENS, FF), 1.0, 6.0, ((0, 32), (1, 16))),
        "out_factors": bell_draw(arg_keys[2], (QUERIES * RANK, FF), (FF * RANK) ** -0.5, 0.005859375, ((0, 32), (1, 16))),
        "in_factors": bell_draw(arg_keys[3], (QUERIES * RANK, D), D ** -0.5, 0.0625, ((0, 32), (1, 16))),
        "basis": bell_draw(arg_keys[4], (D, D), D ** -0.5, 0.0625, ((0, 16), (1, 32))),
        "eigvals": jnp.clip(jnp.exp(math.log(10.0) - 4.6051702 * jax.random.uniform(arg_keys[5], (D,), jnp.float32) ** level_of(arg_keys[5], (D,), ((0, 32),), -0.2, 0.2)), 0.1, 10.0),
    }


DAMP = 0.01


def project_rows(token_rows, factors):
    return lax.dot_general(token_rows, factors, (((1,), (1,)), ((), ())), preferred_element_type=jnp.float32)


def reference(activations, output_grads, out_factors, in_factors, basis, eigvals):
    rotated = jnp.dot(in_factors, basis, preferred_element_type=jnp.float32)
    scaled = (rotated / (eigvals + DAMP)[None, :]).astype(jnp.bfloat16)
    precond = lax.dot_general(scaled, basis, (((1,), (1,)), ((), ())), preferred_element_type=jnp.float32).astype(jnp.bfloat16)
    act_blocks = activations.reshape(N_DP, TOK_DEV, D)
    grad_blocks = output_grads.reshape(N_DP, TOK_DEV, FF)

    def score_block(pair):
        input_side = project_rows(pair[0], precond)
        output_side = project_rows(pair[1], out_factors)
        paired = (input_side * output_side).reshape(TOK_DEV, QUERIES, RANK)
        return jnp.sum(paired, axis=2)

    scores = lax.map(score_block, (act_blocks, grad_blocks))
    return scores.reshape(TOKENS, QUERIES)
```

```python
import jax
import jax.numpy as jnp
from jax import lax
from jax.experimental import pallas as pl
from jax.experimental.pallas import tpu as pltpu
from jax.sharding import Mesh, PartitionSpec as P

RANK = 32
DAMP = 0.01

X, ZL, ZH, Y, C = 4, 8, 2, 4, 2
BF = jnp.bfloat16
F32 = jnp.float32


def from_next(v, axis, by):
    n = lax.axis_size(axis)
    return lax.ppermute(v, axis, [(i, (i - by) % n) for i in range(n)])


def from_xor(v, axis, bit):
    return lax.ppermute(v, axis, [(i, i ^ bit) for i in range(lax.axis_size(axis))])


def scatter(v, axis):
    return lax.all_to_all(v, axis, 0, 0, tiled=True)


def gather(v, axis):
    return scatter(jnp.broadcast_to(v[None], (lax.axis_size(axis),) + v.shape), axis)


def out_kernel(pos, g_ref, o0, o1, o2, o3, out_ref, rows):
    x, zl, y, c = pos[0], pos[1], pos[2], pos[3]
    order = (0, 4, 2, 6, 1, 5, 3, 7)
    for dx, src in enumerate((o0, o1, o2, o3)):
        at_x = lax.rem(x + dx, X)
        for slot, j in enumerate(order):
            owner = jnp.bitwise_xor(zl, j)
            dy = lax.rem(lax.div(owner, 2) - y + Y, Y)
            dc = jnp.bitwise_xor(jnp.bitwise_and(owner, 1), c)
            dst = ((dc * Y + dy) * X + at_x) * RANK
            rows[pl.ds(pl.multiple_of(dst, RANK), RANK), :] = src[pl.ds(slot * RANK, RANK), :]

    @pl.loop(0, 4)
    def _(i):
        at = pl.ds(pl.multiple_of(i * 256, 256), 256)
        out_ref[at, :] = lax.dot_general(
            rows[at, :], g_ref[...], (((1,), (1,)), ((), ())), preferred_element_type=F32
        )


def output_part(pos, output_grads, blocks):
    ff = output_grads.shape[1]
    vmem = pl.BlockSpec(memory_space=pltpu.VMEM)
    return pl.pallas_call(
        out_kernel,
        out_shape=jax.ShapeDtypeStruct((1024, 256), F32),
        in_specs=[pl.BlockSpec(memory_space=pltpu.SMEM)] + [vmem] * 5,
        out_specs=vmem,
        scratch_shapes=[pltpu.VMEM((1024, ff), BF)],
        compiler_params=pltpu.CompilerParams(vmem_limit_bytes=24 * 2**20),
        cost_estimate=pl.CostEstimate(
            flops=2 * 1024 * 256 * ff, bytes_accessed=2 * 1280 * ff + 4 * 1024 * 256, transcendentals=0
        ),
    )(pos, output_grads, *blocks)


def on_device(activations, output_grads, out_factors, in_factors, basis, eigvals):
    x, zl = lax.axis_index("x"), lax.axis_index("zl")
    y, c = lax.axis_index("y"), lax.axis_index("c")

    both = jnp.concatenate([basis, activations[:, :256], activations[:, 256:]], axis=0)
    over_y = jnp.stack([both] + [from_next(both, "y", s) for s in (1, 2, 3)])
    over_c = jnp.stack([over_y, from_xor(over_y, "c", 1)])
    basis_all = over_c[:, :, :512].reshape(4096, 256)
    acts_all = over_c[:, :, 512:].reshape(16, 256, 256).transpose(1, 0, 2).reshape(256, 4096)

    f8 = scatter(gather(in_factors, "zl"), ("y", "c"))
    f_here = jnp.concatenate(
        [
            lax.dynamic_index_in_dim(f8, ((y + dy) % Y) * 2 + (c ^ dc), 0, keepdims=False)
            for dc in (0, 1)
            for dy in range(Y)
        ],
        axis=1,
    )
    f_all = gather(f_here, "x").reshape(128, 4096)
    rot = jnp.dot(f_all, basis_all, preferred_element_type=F32)
    rotated = rot + from_xor(rot, "zh", 1)
    scaled = (rotated / (eigvals + DAMP)[None, :]).astype(BF)

    pt = lax.dot_general(basis_all, scaled, (((1,), (1,)), ((), ())), preferred_element_type=F32)
    s1 = jnp.sum(scatter(pt.astype(BF).reshape(X, 1024, 128), "x").astype(F32), axis=0)
    s2 = jnp.sum(scatter(s1.astype(BF).reshape(ZL, 128, 128), "zl").astype(F32), axis=0)
    precond = gather(gather(s2.astype(BF), "zl").reshape(1024, 128), "x").reshape(4096, 128)
    input_side = jnp.dot(acts_all, precond, preferred_element_type=F32)

    o = out_factors
    for bit in (4, 2, 1):
        o = jnp.concatenate([o, from_xor(o, "zl", bit)], axis=0)
    blocks = [o] + [from_next(o, "x", s) for s in (1, 2, 3)]
    pos = jnp.stack([x, zl, y, c]).astype(jnp.int32)
    part = output_part(pos, output_grads, blocks)
    part = part[:512] + from_xor(part[512:], "c", 1)
    part = part[:128] + sum(from_next(part[s * 128:(s + 1) * 128], "y", -s) for s in (1, 2, 3))
    output_side = part + from_xor(part, "zh", 1)

    paired = input_side.T * output_side
    shares = jnp.sum(paired.reshape(X, RANK, 256), axis=1)
    pieces = shares.reshape(X, 16, 16).transpose(1, 0, 2)
    got = scatter(pieces, ("zh", "y", "c")).reshape(ZH, Y * C, X, 16)
    return jnp.sum(got, axis=0).transpose(2, 1, 0).reshape(16, X * ZL)


def solution(mesh):
    fine = Mesh(mesh.devices.reshape(X, ZL, ZH, Y, C), ("x", "zl", "zh", "y", "c"))
    dp, feats = ("x", "zl"), ("zh", "y", "c")
    return jax.shard_map(
        on_device,
        mesh=fine,
        in_specs=(P(dp, feats), P(dp, feats), P(dp, feats), P(dp, feats), P(feats, dp), P(dp)),
        out_specs=P(dp + feats, None),
        check_vma=False,
    )
```

```python
import jax
import jax.numpy as jnp
from jax import lax
from jax.experimental import pallas as pl
from jax.experimental.pallas import tpu as pltpu
from jax.sharding import Mesh, PartitionSpec as P

RANK = 32
DAMP = 0.01

X, ZL, ZH, Y, C = 4, 8, 2, 4, 2
BF = jnp.bfloat16
F32 = jnp.float32
KB = RANK // (Y * C)
XOR_ORDER = (0, 4, 2, 6, 1, 5, 3, 7)
VMEM = pl.BlockSpec(memory_space=pltpu.VMEM)
SMEM = pl.BlockSpec(memory_space=pltpu.SMEM)


def swap(v, axis, partner):
    return lax.ppermute(v, axis, [(i, partner(i)) for i in range(lax.axis_size(axis))])


def scatter(v, axis):
    return lax.all_to_all(v, axis, 0, 0, tiled=True)


def gather(v, axis):
    return scatter(jnp.broadcast_to(v[None], (lax.axis_size(axis),) + v.shape), axis)


def after(v, *others):
    return lax.optimization_barrier((v,) + others)[0]


def call(kernel, out, args, specs, flops, scratch=(), limit=24):
    many = isinstance(out, list)
    moved = sum(a.size * a.dtype.itemsize for a in args)
    return pl.pallas_call(
        kernel,
        out_shape=out,
        in_specs=specs,
        out_specs=[VMEM] * len(out) if many else VMEM,
        scratch_shapes=scratch,
        compiler_params=pltpu.CompilerParams(vmem_limit_bytes=limit * 2**20),
        cost_estimate=pl.CostEstimate(flops=flops, bytes_accessed=moved, transcendentals=0),
    )(*args)


def rotate_kernel(f, basis, rot):
    rows = jnp.concatenate(
        [jnp.concatenate([f[zl * Y * C + s] for zl in range(ZL)], axis=0) for s in range(Y * C)], axis=1
    )
    for i in range(X):
        for h in range(2):
            at = (i * 2 + h) * 128
            b = jnp.concatenate([basis[s, at:at + 128, :] for s in range(Y * C)], axis=0)
            rot[i, :, h * 128:(h + 1) * 128] = jnp.dot(rows, b, preferred_element_type=F32)


def precond_kernel(scaled, basis, pt):
    eigs = jnp.concatenate([scaled[i] for i in range(X)], axis=1)
    for s in range(Y * C):
        b = jnp.concatenate([basis[s, j * 128:(j + 1) * 128, :] for j in range(2 * X)], axis=1)
        pt[s] = lax.dot_general(b, eigs, (((1,), (1,)), ((), ())), preferred_element_type=F32).astype(BF)


def input_kernel(acts, pt, ins):
    p = jnp.concatenate([pt[s] for s in range(Y * C)], axis=0)
    for i in range(X):
        a = jnp.concatenate([acts[s, i * 256:(i + 1) * 256, :] for s in range(Y * C)], axis=1)
        ins[i] = jnp.dot(a, p, preferred_element_type=F32)


def output_kernel(pos, g0, g1, o0, o1, part, rows):
    for dx, held in enumerate((o0, o1)):
        low = jnp.bitwise_and(jnp.bitwise_xor(pos[0], dx), 1)
        for slot, j in enumerate(XOR_ORDER):
            dst = (jnp.bitwise_xor(pos[4], j) * 2 + low) * RANK
            rows[pl.ds(pl.multiple_of(dst, RANK), RANK), :] = held[slot * RANK:(slot + 1) * RANK, :]
    for i, g in enumerate((g0, g1)):
        both = lax.dot_general(rows[...], g[...], (((1,), (1,)), ((), ())), preferred_element_type=F32)
        for b in range(Y * C):
            dc = jnp.bitwise_xor(pos[3], b % C)
            dy = lax.rem(b // C - pos[2] + Y, Y)
            for q in range(2 * ZL):
                src = q * RANK + b * KB
                part[dc * Y + dy, q * KB:(q + 1) * KB, i * 256:(i + 1) * 256] = both[src:src + KB, :]


def sides_kernel(pos, parts, out_own, out_partner, keep, send):
    ins = (parts[0] + parts[1] + parts[2] + parts[3]).T
    a, b = out_own[...], out_partner[...]
    low_x = pos[0] < 2
    low, high = jnp.where(low_x, a, b), jnp.where(low_x, b, a)
    n = 2 * KB
    outs = jnp.concatenate(
        [v[zl * n:(zl + 1) * n, :] for zl in range(ZL) for v in (low, high)], axis=0
    )
    first = pos[1] == 0
    for i, v in enumerate((ins, outs)):
        keep[i] = jnp.where(first, v[:, :128], v[:, 128:])
        send[i] = jnp.where(first, v[:, 128:], v[:, :128])


def from_next(v, axis, by):
    n = lax.axis_size(axis)
    return lax.ppermute(v, axis, [(i, (i - by) % n) for i in range(n)])


def on_device(activations, output_grads, out_factors, in_factors, basis, eigvals):
    x, zl, zh = lax.axis_index("x"), lax.axis_index("zl"), lax.axis_index("zh")
    pos = jnp.stack([x, zh, lax.axis_index("y"), lax.axis_index("c"), zl])
    ff = output_grads.shape[1]

    mix = jnp.concatenate(
        [
            in_factors.reshape(RANK, X, 128).transpose(1, 0, 2),
            activations.reshape(256, X, 128).transpose(1, 0, 2),
            basis.reshape(X, 128, 2, 128).transpose(0, 2, 1, 3).reshape(X, 256, 128),
        ],
        axis=1,
    )
    mix = scatter(mix, "x")
    basis_all = lax.all_gather(mix[:, 288:].reshape(1024, 128), ("y", "c"))
    acts_all = lax.all_gather(mix[:, 32:288].reshape(1024, 128), ("y", "c"))
    o_in = swap(out_factors, "zl", lambda i: i ^ 4)

    f = mix[:, :32].reshape(X, Y * C, KB, 128).transpose(1, 0, 2, 3).reshape(1, Y * C, X * KB, 128)
    f = jnp.broadcast_to(f, (ZL, Y * C, X * KB, 128)).reshape(ZL * Y * C, X * KB, 128)
    grads_partner = swap(after(output_grads, f), "x", lambda i: 3 - i)
    f = scatter(f, ("zl", "y", "c"))

    rot = call(
        rotate_kernel, jax.ShapeDtypeStruct((X, 128, 256), F32), [f, basis_all], [VMEM] * 2, 2 * 128 * 1024 * 1024
    )
    rx = after(scatter(rot, "x"), grads_partner)
    o = jnp.concatenate([after(out_factors, rot), o_in], axis=0)
    o_in = swap(o, "zl", lambda i: i ^ 2)
    rot = jnp.sum(rx, axis=0)
    rotated = rot + after(swap(rot, "zh", lambda i: 1 - i), o_in)
    o = jnp.concatenate([after(o, rx), o_in], axis=0)
    o_in = swap(o, "zl", lambda i: i ^ 1)
    scaled = (rotated / (eigvals + DAMP)[None, :]).astype(BF)
    scaled = gather(scaled, "x")
    pt = call(
        precond_kernel, jax.ShapeDtypeStruct((Y * C, 128, 128), BF), [scaled, basis_all], [VMEM] * 2, 2 * 128 * 1024 * 1024
    )

    r2 = scatter(pt, "zl")
    o = jnp.concatenate([after(o, scaled), o_in], axis=0)
    o_other = swap(o, "x", lambda i: i ^ 1)

    part = call(
        output_kernel,
        jax.ShapeDtypeStruct((Y * C, 2 * ZL * KB, 512), F32),
        [pos, output_grads, grads_partner, after(o, pt), o_other],
        [SMEM] + [VMEM] * 4,
        2 * 512 * 512 * ff,
        [pltpu.VMEM((512, ff), BF)],
    )
    part = part[:Y] + swap(part[Y:], "c", lambda i: 1 - i)
    r2 = after(r2, part)
    s2 = jnp.sum(r2.astype(F32), axis=0).astype(BF)
    part = part[0] + sum(from_next(part[s], "y", -s) for s in (1, 2, 3))
    precond = after(gather(s2, "zl"), part)
    out_partner = swap(part[:, 256:], "x", lambda i: 3 - i)

    ins = call(
        input_kernel, jax.ShapeDtypeStruct((X, 256, 128), F32), [acts_all, precond], [VMEM] * 2, 2 * 128 * 1024 * 1024
    )
    keep, send = call(
        sides_kernel,
        [jax.ShapeDtypeStruct((2, 128, 128), F32)] * 2,
        [pos, scatter(ins, "x"), part[:, :256], out_partner],
        [SMEM] + [VMEM] * 3,
        128 * 1024,
    )
    sides = keep + swap(send, "zh", lambda i: 1 - i)
    shares = jnp.sum((sides[0] * sides[1]).reshape(ZL * X, KB, 128), axis=1)
    pieces = shares.reshape(ZL, X, Y * C, 16).transpose(2, 3, 1, 0).reshape(Y * C, 16 * X * ZL)
    return jnp.sum(scatter(pieces, ("y", "c")), axis=0).reshape(16, X * ZL)


def solution(mesh):
    fine = Mesh(mesh.devices.reshape(X, ZL, ZH, Y, C), ("x", "zl", "zh", "y", "c"))
    dp, feats = ("x", "zl"), ("zh", "y", "c")
    return jax.shard_map(
        on_device,
        mesh=fine,
        in_specs=(P(dp, feats), P(dp, feats), P(dp, feats), P(dp, feats), P(feats, dp), P(dp)),
        out_specs=P(dp + feats, None),
        check_vma=False,
    )
```

```python
import jax
import jax.numpy as jnp
from jax import lax
from jax.experimental import pallas as pl
from jax.experimental.pallas import tpu as pltpu
from jax.sharding import Mesh, PartitionSpec as P

RANK = 32
DAMP = 0.01

X, ZL, ZH, Y, C = 4, 8, 2, 4, 2
BF = jnp.bfloat16
F32 = jnp.float32
KB = RANK // (Y * C)
XOR_ORDER = (0, 4, 2, 6, 1, 5, 3, 7)
VMEM = pl.BlockSpec(memory_space=pltpu.VMEM)
SMEM = pl.BlockSpec(memory_space=pltpu.SMEM)


def swap(v, axis, partner):
    return lax.ppermute(v, axis, [(i, partner(i)) for i in range(lax.axis_size(axis))])


def scatter(v, axis):
    return lax.all_to_all(v, axis, 0, 0, tiled=True)


def gather(v, axis):
    return scatter(jnp.broadcast_to(v[None], (lax.axis_size(axis),) + v.shape), axis)


def after(v, *others):
    return lax.optimization_barrier((v,) + others)[0]


def call(kernel, out, args, specs, flops, scratch=(), limit=24):
    many = isinstance(out, list)
    moved = sum(a.size * a.dtype.itemsize for a in args)
    return pl.pallas_call(
        kernel,
        out_shape=out,
        in_specs=specs,
        out_specs=[VMEM] * len(out) if many else VMEM,
        scratch_shapes=scratch,
        compiler_params=pltpu.CompilerParams(vmem_limit_bytes=limit * 2**20),
        cost_estimate=pl.CostEstimate(flops=flops, bytes_accessed=moved, transcendentals=0),
    )(*args)


def cut_kernel(factors, acts, basis, mix):
    for i in range(X):
        q = slice(i * 128, (i + 1) * 128)
        mix[i, :32, :] = factors[:, q]
        mix[i, 32:288, :] = acts[:, q]
        for h in range(2):
            mix[i, 288 + h * 128:416 + h * 128, :] = basis[q, h * 128:(h + 1) * 128]


def spread_kernel(mix, out):
    rows = [mix[i, :32, :].astype(F32) for i in range(X)]
    for b in range(Y * C):
        piece = jnp.concatenate([v[b * KB:(b + 1) * KB, :] for v in rows], axis=0).astype(BF)
        for zl in range(ZL):
            out[zl * Y * C + b] = piece


def rotate_kernel(f, basis, rot):
    rows = jnp.concatenate(
        [jnp.concatenate([f[zl * Y * C + s] for zl in range(ZL)], axis=0) for s in range(Y * C)], axis=1
    )
    for i in range(X):
        for h in range(2):
            at = (i * 2 + h) * 128
            b = jnp.concatenate([basis[s, at:at + 128, :] for s in range(Y * C)], axis=0)
            rot[i, :, h * 128:(h + 1) * 128] = jnp.dot(rows, b, preferred_element_type=F32)


def precond_kernel(scaled, basis, pt):
    eigs = jnp.concatenate([scaled[i] for i in range(X)], axis=1)
    for s in range(Y * C):
        b = jnp.concatenate([basis[s, j * 128:(j + 1) * 128, :] for j in range(2 * X)], axis=1)
        pt[s] = lax.dot_general(b, eigs, (((1,), (1,)), ((), ())), preferred_element_type=F32).astype(BF)


def input_kernel(acts, pt, ins):
    p = jnp.concatenate([pt[s] for s in range(Y * C)], axis=0)
    for i in range(X):
        a = jnp.concatenate([acts[s, i * 256:(i + 1) * 256, :] for s in range(Y * C)], axis=1)
        ins[i] = jnp.dot(a, p, preferred_element_type=F32)


def output_kernel(pos, g0, g1, o0, o1, part, rows):
    for dx, held in enumerate((o0, o1)):
        low = jnp.bitwise_and(jnp.bitwise_xor(pos[0], dx), 1)
        for slot, j in enumerate(XOR_ORDER):
            dst = (jnp.bitwise_xor(pos[4], j) * 2 + low) * RANK
            rows[pl.ds(pl.multiple_of(dst, RANK), RANK), :] = held[slot * RANK:(slot + 1) * RANK, :]
    for i, g in enumerate((g0, g1)):
        both = lax.dot_general(rows[...], g[...], (((1,), (1,)), ((), ())), preferred_element_type=F32)
        for b in range(Y * C):
            dc = jnp.bitwise_xor(pos[3], b % C)
            dy = lax.rem(b // C - pos[2] + Y, Y)
            for q in range(2 * ZL):
                src = q * RANK + b * KB
                part[dc * Y + dy, q * KB:(q + 1) * KB, i * 256:(i + 1) * 256] = both[src:src + KB, :]


def sides_kernel(pos, parts, out_own, out_partner, keep, send):
    ins = (parts[0] + parts[1] + parts[2] + parts[3]).T
    a, b = out_own[...], out_partner[...]
    low_x = pos[0] < 2
    low, high = jnp.where(low_x, a, b), jnp.where(low_x, b, a)
    n = 2 * KB
    outs = jnp.concatenate(
        [v[zl * n:(zl + 1) * n, :] for zl in range(ZL) for v in (low, high)], axis=0
    )
    first = pos[1] == 0
    for i, v in enumerate((ins, outs)):
        keep[i] = jnp.where(first, v[:, :128], v[:, 128:])
        send[i] = jnp.where(first, v[:, 128:], v[:, :128])


def from_next(v, axis, by):
    n = lax.axis_size(axis)
    return lax.ppermute(v, axis, [(i, (i - by) % n) for i in range(n)])


def on_device(activations, output_grads, out_factors, in_factors, basis, eigvals):
    x, zl, zh = lax.axis_index("x"), lax.axis_index("zl"), lax.axis_index("zh")
    pos = jnp.stack([x, zh, lax.axis_index("y"), lax.axis_index("c"), zl])
    ff = output_grads.shape[1]

    mix = call(
        cut_kernel, jax.ShapeDtypeStruct((X, 544, 128), BF), [in_factors, activations, basis], [VMEM] * 3, 0
    )
    mix = scatter(mix, "x")
    basis_all = lax.all_gather(mix[:, 288:].reshape(1024, 128), ("y", "c"))
    acts_all = lax.all_gather(mix[:, 32:288].reshape(1024, 128), ("y", "c"))
    o_in = swap(out_factors, "zl", lambda i: i ^ 4)

    f = call(spread_kernel, jax.ShapeDtypeStruct((ZL * Y * C, X * KB, 128), BF), [mix], [VMEM], 0)
    grads_partner = swap(after(output_grads, f), "x", lambda i: 3 - i)
    f = scatter(f, ("zl", "y", "c"))

    rot = call(
        rotate_kernel, jax.ShapeDtypeStruct((X, 128, 256), F32), [f, basis_all], [VMEM] * 2, 2 * 128 * 1024 * 1024
    )
    rx = after(scatter(rot, "x"), grads_partner)
    o = jnp.concatenate([after(out_factors, rot), o_in], axis=0)
    o_in = swap(o, "zl", lambda i: i ^ 2)
    rot = jnp.sum(rx, axis=0)
    rotated = rot + after(swap(rot, "zh", lambda i: 1 - i), o_in)
    o = jnp.concatenate([after(o, rx), o_in], axis=0)
    o_in = swap(o, "zl", lambda i: i ^ 1)
    scaled = (rotated / (eigvals + DAMP)[None, :]).astype(BF)
    scaled = gather(scaled, "x")
    pt = call(
        precond_kernel, jax.ShapeDtypeStruct((Y * C, 128, 128), BF), [scaled, basis_all], [VMEM] * 2, 2 * 128 * 1024 * 1024
    )

    r2 = scatter(pt, "zl")
    o = jnp.concatenate([after(o, scaled), o_in], axis=0)
    o_other = swap(o, "x", lambda i: i ^ 1)

    part = call(
        output_kernel,
        jax.ShapeDtypeStruct((Y * C, 2 * ZL * KB, 512), F32),
        [pos, output_grads, grads_partner, after(o, pt), o_other],
        [SMEM] + [VMEM] * 4,
        2 * 512 * 512 * ff,
        [pltpu.VMEM((512, ff), BF)],
    )
    part = part[:Y] + swap(part[Y:], "c", lambda i: 1 - i)
    r2 = after(r2, part)
    s2 = jnp.sum(r2.astype(F32), axis=0).astype(BF)
    part = part[0] + sum(from_next(part[s], "y", -s) for s in (1, 2, 3))
    precond = after(gather(s2, "zl"), part, acts_all)
    out_partner = swap(part[:, 256:], "x", lambda i: 3 - i)

    ins = call(
        input_kernel, jax.ShapeDtypeStruct((X, 256, 128), F32), [acts_all, precond], [VMEM] * 2, 2 * 128 * 1024 * 1024
    )
    keep, send = call(
        sides_kernel,
        [jax.ShapeDtypeStruct((2, 128, 128), F32)] * 2,
        [pos, scatter(ins, "x"), part[:, :256], out_partner],
        [SMEM] + [VMEM] * 3,
        128 * 1024,
    )
    sides = keep + swap(send, "zh", lambda i: 1 - i)
    shares = jnp.sum((sides[0] * sides[1]).reshape(ZL * X, KB, 128), axis=1)
    pieces = shares.reshape(ZL, X, Y * C, 16).transpose(2, 3, 1, 0).reshape(Y * C, 16 * X * ZL)
    return jnp.sum(scatter(pieces, ("y", "c")), axis=0).reshape(16, X * ZL)


def solution(mesh):
    fine = Mesh(mesh.devices.reshape(X, ZL, ZH, Y, C), ("x", "zl", "zh", "y", "c"))
    dp, feats = ("x", "zl"), ("zh", "y", "c")
    return jax.shard_map(
        on_device,
        mesh=fine,
        in_specs=(P(dp, feats), P(dp, feats), P(dp, feats), P(dp, feats), P(feats, dp), P(dp)),
        out_specs=P(dp + feats, None),
        check_vma=False,
    )
```

```python
import jax
import jax.numpy as jnp
from jax import lax
from jax.experimental import pallas as pl
from jax.experimental.pallas import tpu as pltpu
from jax.sharding import Mesh, PartitionSpec as P

RANK = 32
DAMP = 0.01

X, ZL, ZH, Y, C = 4, 8, 2, 4, 2
BF = jnp.bfloat16
F32 = jnp.float32
KB = RANK // (Y * C)
XOR_ORDER = (0, 4, 2, 6, 1, 5, 3, 7)
VMEM = pl.BlockSpec(memory_space=pltpu.VMEM)
SMEM = pl.BlockSpec(memory_space=pltpu.SMEM)
ANY = pl.BlockSpec(memory_space=pl.ANY)


def swap(v, axis, partner):
    return lax.ppermute(v, axis, [(i, partner(i)) for i in range(lax.axis_size(axis))])


def scatter(v, axis):
    return lax.all_to_all(v, axis, 0, 0, tiled=True)


def gather(v, axis):
    return scatter(jnp.broadcast_to(v[None], (lax.axis_size(axis),) + v.shape), axis)


def after(v, *others):
    return lax.optimization_barrier((v,) + others)[0]


def call(kernel, out, args, specs, flops, scratch=(), limit=24):
    many = isinstance(out, list)
    moved = sum(a.size * a.dtype.itemsize for a in args)
    return pl.pallas_call(
        kernel,
        out_shape=out,
        in_specs=specs,
        out_specs=[VMEM] * len(out) if many else VMEM,
        scratch_shapes=scratch,
        compiler_params=pltpu.CompilerParams(vmem_limit_bytes=limit * 2**20),
        cost_estimate=pl.CostEstimate(flops=flops, bytes_accessed=moved, transcendentals=0),
    )(*args)


def cut_kernel(factors, acts, basis, mix, sems):
    pairs = []
    for i in range(X):
        q = pl.ds(i * 128, 128)
        pairs.append((acts.at[:, q], mix.at[i, pl.ds(32, 256), :]))
        for h in range(2):
            pairs.append((basis.at[q, pl.ds(h * 128, 128)], mix.at[i, pl.ds(288 + h * 128, 128), :]))
        pairs.append((factors.at[:, q], mix.at[i, pl.ds(0, 32), :]))
    copies = [pltpu.make_async_copy(src, dst, sems.at[n]) for n, (src, dst) in enumerate(pairs)]
    for copy in copies:
        copy.start()
    for copy in copies:
        copy.wait()


def spread_kernel(mix, out):
    rows = [mix[i, :32, :].astype(F32) for i in range(X)]
    for b in range(Y * C):
        piece = jnp.concatenate([v[b * KB:(b + 1) * KB, :] for v in rows], axis=0).astype(BF)
        for zl in range(ZL):
            out[zl * Y * C + b] = piece


def fetch_quarters(src, held, sems):
    copies = [
        pltpu.make_async_copy(src.at[:, pl.ds(i * 256, 256), :], held.at[i], sems.at[i]) for i in range(X)
    ]
    for copy in copies:
        copy.start()
    return copies


def rotate_kernel(f, basis, rot, held, sems):
    copies = fetch_quarters(basis, held, sems)
    rows = jnp.concatenate(
        [jnp.concatenate([f[zl * Y * C + s] for zl in range(ZL)], axis=0) for s in range(Y * C)], axis=1
    )
    for i in range(X):
        copies[i].wait()
        for h in range(2):
            b = jnp.concatenate([held[i, s, h * 128:(h + 1) * 128, :] for s in range(Y * C)], axis=0)
            rot[i, :, h * 128:(h + 1) * 128] = jnp.dot(rows, b, preferred_element_type=F32)


def precond_kernel(scaled, basis, pt):
    eigs = jnp.concatenate([scaled[i] for i in range(X)], axis=1)
    for s in range(Y * C):
        b = jnp.concatenate([basis[s, j * 128:(j + 1) * 128, :] for j in range(2 * X)], axis=1)
        pt[s] = lax.dot_general(b, eigs, (((1,), (1,)), ((), ())), preferred_element_type=F32).astype(BF)


def input_kernel(acts, pt, ins, held, sems):
    copies = fetch_quarters(acts, held, sems)
    p = jnp.concatenate([pt[s] for s in range(Y * C)], axis=0)
    for i in range(X):
        copies[i].wait()
        a = jnp.concatenate([held[i, s] for s in range(Y * C)], axis=1)
        ins[i] = jnp.dot(a, p, preferred_element_type=F32)


def output_kernel(pos, g0, g1, o0, o1, part, rows):
    for dx, held in enumerate((o0, o1)):
        low = jnp.bitwise_and(jnp.bitwise_xor(pos[0], dx), 1)
        for slot, j in enumerate(XOR_ORDER):
            dst = (jnp.bitwise_xor(pos[4], j) * 2 + low) * RANK
            rows[pl.ds(pl.multiple_of(dst, RANK), RANK), :] = held[slot * RANK:(slot + 1) * RANK, :]
    for i, g in enumerate((g0, g1)):
        both = lax.dot_general(rows[...], g[...], (((1,), (1,)), ((), ())), preferred_element_type=F32)
        for b in range(Y * C):
            dc = jnp.bitwise_xor(pos[3], b % C)
            dy = lax.rem(b // C - pos[2] + Y, Y)
            for q in range(2 * ZL):
                src = q * RANK + b * KB
                part[dc * Y + dy, q * KB:(q + 1) * KB, i * 256:(i + 1) * 256] = both[src:src + KB, :]


def sides_kernel(pos, parts, out_own, out_partner, keep, send):
    ins = (parts[0] + parts[1] + parts[2] + parts[3]).T
    a, b = out_own[...], out_partner[...]
    low_x = pos[0] < 2
    low, high = jnp.where(low_x, a, b), jnp.where(low_x, b, a)
    n = 2 * KB
    outs = jnp.concatenate(
        [v[zl * n:(zl + 1) * n, :] for zl in range(ZL) for v in (low, high)], axis=0
    )
    first = pos[1] == 0
    for i, v in enumerate((ins, outs)):
        keep[i] = jnp.where(first, v[:, :128], v[:, 128:])
        send[i] = jnp.where(first, v[:, 128:], v[:, :128])


def from_next(v, axis, by):
    n = lax.axis_size(axis)
    return lax.ppermute(v, axis, [(i, (i - by) % n) for i in range(n)])


def on_device(activations, output_grads, out_factors, in_factors, basis, eigvals):
    x, zl, zh = lax.axis_index("x"), lax.axis_index("zl"), lax.axis_index("zh")
    pos = jnp.stack([x, zh, lax.axis_index("y"), lax.axis_index("c"), zl])
    ff = output_grads.shape[1]

    mix = call(
        cut_kernel, jax.ShapeDtypeStruct((X, 544, 128), BF), [in_factors, activations, basis], [ANY] * 3, 0,
        [pltpu.SemaphoreType.DMA((4 * X,))],
    )
    mix = scatter(mix, "x")
    basis_all = lax.all_gather(mix[:, 288:].reshape(1024, 128), ("y", "c"))
    acts_all = lax.all_gather(mix[:, 32:288].reshape(1024, 128), ("y", "c"))
    o_in = swap(out_factors, "zl", lambda i: i ^ 4)

    f = call(spread_kernel, jax.ShapeDtypeStruct((ZL * Y * C, X * KB, 128), BF), [mix], [VMEM], 0)
    grads_partner = swap(after(output_grads, f), "x", lambda i: 3 - i)
    f = scatter(f, ("zl", "y", "c"))

    quarters = [pltpu.VMEM((X, Y * C, 256, 128), BF), pltpu.SemaphoreType.DMA((X,))]
    rot = call(
        rotate_kernel, jax.ShapeDtypeStruct((X, 128, 256), F32), [f, basis_all], [VMEM, ANY],
        2 * 128 * 1024 * 1024, quarters,
    )
    rx = after(scatter(rot, "x"), grads_partner)
    o = jnp.concatenate([after(out_factors, rot), o_in], axis=0)
    o_in = swap(o, "zl", lambda i: i ^ 2)
    rot = jnp.sum(rx, axis=0)
    rotated = rot + after(swap(rot, "zh", lambda i: 1 - i), o_in)
    o = jnp.concatenate([after(o, rx), o_in], axis=0)
    o_in = swap(o, "zl", lambda i: i ^ 1)
    scaled = (rotated / (eigvals + DAMP)[None, :]).astype(BF)
    scaled = gather(scaled, "x")
    pt = call(
        precond_kernel, jax.ShapeDtypeStruct((Y * C, 128, 128), BF), [scaled, basis_all], [VMEM] * 2, 2 * 128 * 1024 * 1024
    )

    r2 = scatter(pt, "zl")
    o = jnp.concatenate([after(o, scaled), o_in], axis=0)
    o_other = swap(o, "x", lambda i: i ^ 1)

    part = call(
        output_kernel,
        jax.ShapeDtypeStruct((Y * C, 2 * ZL * KB, 512), F32),
        [pos, output_grads, grads_partner, after(o, pt), o_other],
        [SMEM] + [VMEM] * 4,
        2 * 512 * 512 * ff,
        [pltpu.VMEM((512, ff), BF)],
    )
    part = part[:Y] + swap(part[Y:], "c", lambda i: 1 - i)
    r2 = after(r2, part)
    s2 = jnp.sum(r2.astype(F32), axis=0).astype(BF)
    part = part[0] + sum(from_next(part[s], "y", -s) for s in (1, 2, 3))
    precond = after(gather(s2, "zl"), part, acts_all)
    out_partner = swap(part[:, 256:], "x", lambda i: 3 - i)

    ins = call(
        input_kernel, jax.ShapeDtypeStruct((X, 256, 128), F32), [acts_all, precond], [ANY, VMEM],
        2 * 128 * 1024 * 1024, quarters,
    )
    keep, send = call(
        sides_kernel,
        [jax.ShapeDtypeStruct((2, 128, 128), F32)] * 2,
        [pos, scatter(ins, "x"), part[:, :256], out_partner],
        [SMEM] + [VMEM] * 3,
        128 * 1024,
    )
    sides = keep + swap(send, "zh", lambda i: 1 - i)
    shares = jnp.sum((sides[0] * sides[1]).reshape(ZL * X, KB, 128), axis=1)
    pieces = shares.reshape(ZL, X, Y * C, 16).transpose(2, 3, 1, 0).reshape(Y * C, 16 * X * ZL)
    return jnp.sum(scatter(pieces, ("y", "c")), axis=0).reshape(16, X * ZL)


def solution(mesh):
    fine = Mesh(mesh.devices.reshape(X, ZL, ZH, Y, C), ("x", "zl", "zh", "y", "c"))
    dp, feats = ("x", "zl"), ("zh", "y", "c")
    return jax.shard_map(
        on_device,
        mesh=fine,
        in_specs=(P(dp, feats), P(dp, feats), P(dp, feats), P(dp, feats), P(feats, dp), P(dp)),
        out_specs=P(dp + feats, None),
        check_vma=False,
    )
```

```python
import jax
import jax.numpy as jnp
from jax import lax
from jax.experimental import pallas as pl
from jax.experimental.pallas import tpu as pltpu
from jax.sharding import Mesh, PartitionSpec as P

RANK = 32
DAMP = 0.01

X, ZL, ZH, Y, C = 4, 8, 2, 4, 2
BF = jnp.bfloat16
F32 = jnp.float32
KB = RANK // (Y * C)
XOR_ORDER = (0, 4, 2, 6, 1, 5, 3, 7)
VMEM = pl.BlockSpec(memory_space=pltpu.VMEM)
SMEM = pl.BlockSpec(memory_space=pltpu.SMEM)


def swap(v, axis, partner):
    return lax.ppermute(v, axis, [(i, partner(i)) for i in range(lax.axis_size(axis))])


def scatter(v, axis):
    return lax.all_to_all(v, axis, 0, 0, tiled=True)


def gather(v, axis):
    return scatter(jnp.broadcast_to(v[None], (lax.axis_size(axis),) + v.shape), axis)


def after(v, *others):
    return lax.optimization_barrier((v,) + others)[0]


def call(kernel, out, args, specs, flops, scratch=(), limit=24):
    many = isinstance(out, list)
    moved = sum(a.size * a.dtype.itemsize for a in args)
    return pl.pallas_call(
        kernel,
        out_shape=out,
        in_specs=specs,
        out_specs=[VMEM] * len(out) if many else VMEM,
        scratch_shapes=scratch,
        compiler_params=pltpu.CompilerParams(vmem_limit_bytes=limit * 2**20),
        cost_estimate=pl.CostEstimate(flops=flops, bytes_accessed=moved, transcendentals=0),
    )(*args)


def cut_kernel(factors, acts, basis, mix):
    for i in range(X):
        q = slice(i * 128, (i + 1) * 128)
        mix[i, :32, :] = factors[:, q]
        mix[i, 32:288, :] = acts[:, q]
        for h in range(2):
            mix[i, 288 + h * 128:416 + h * 128, :] = basis[q, h * 128:(h + 1) * 128]


def spread_kernel(mix, out):
    rows = [mix[i, :32, :].astype(F32) for i in range(X)]
    for b in range(Y * C):
        piece = jnp.concatenate([v[b * KB:(b + 1) * KB, :] for v in rows], axis=0).astype(BF)
        for zl in range(ZL):
            out[zl * Y * C + b] = piece


def rotate_kernel(f, basis, rot):
    rows = jnp.concatenate(
        [jnp.concatenate([f[zl * Y * C + s] for zl in range(ZL)], axis=0) for s in range(Y * C)], axis=1
    )
    for i in range(X):
        for h in range(2):
            at = (i * 2 + h) * 128
            b = jnp.concatenate([basis[s, at:at + 128, :] for s in range(Y * C)], axis=0)
            rot[i, :, h * 128:(h + 1) * 128] = jnp.dot(rows, b, preferred_element_type=F32)


def precond_kernel(scaled, basis, pt):
    eigs = jnp.concatenate([scaled[i] for i in range(X)], axis=1)
    for s in range(Y * C):
        b = jnp.concatenate([basis[s, j * 128:(j + 1) * 128, :] for j in range(2 * X)], axis=1)
        pt[s] = lax.dot_general(b, eigs, (((1,), (1,)), ((), ())), preferred_element_type=F32).astype(BF)


def input_kernel(acts, pt, ins):
    p = jnp.concatenate([pt[s] for s in range(Y * C)], axis=0)
    for i in range(X):
        a = jnp.concatenate([acts[s, i * 256:(i + 1) * 256, :] for s in range(Y * C)], axis=1)
        ins[i] = jnp.dot(a, p, preferred_element_type=F32)


def output_kernel(pos, g0, g1, o0, o1, part, rows):
    for dx, held in enumerate((o0, o1)):
        low = jnp.bitwise_and(jnp.bitwise_xor(pos[0], dx), 1)
        for slot, j in enumerate(XOR_ORDER):
            dst = (jnp.bitwise_xor(pos[4], j) * 2 + low) * RANK
            rows[pl.ds(pl.multiple_of(dst, RANK), RANK), :] = held[slot * RANK:(slot + 1) * RANK, :]
    for i, g in enumerate((g0, g1)):
        both = lax.dot_general(rows[...], g[...], (((1,), (1,)), ((), ())), preferred_element_type=F32)
        for b in range(Y * C):
            dc = jnp.bitwise_xor(pos[3], b % C)
            dy = lax.rem(b // C - pos[2] + Y, Y)
            for q in range(2 * ZL):
                src = q * RANK + b * KB
                part[dc * Y + dy, q * KB:(q + 1) * KB, i * 256:(i + 1) * 256] = both[src:src + KB, :]


def sides_kernel(pos, parts, out_own, out_partner, keep, send):
    ins = (parts[0] + parts[1] + parts[2] + parts[3]).T
    a, b = out_own[...], out_partner[...]
    low_x = pos[0] < 2
    low, high = jnp.where(low_x, a, b), jnp.where(low_x, b, a)
    n = 2 * KB
    outs = jnp.concatenate(
        [v[zl * n:(zl + 1) * n, :] for zl in range(ZL) for v in (low, high)], axis=0
    )
    first = pos[1] == 0
    for i, v in enumerate((ins, outs)):
        keep[i] = jnp.where(first, v[:, :128], v[:, 128:])
        send[i] = jnp.where(first, v[:, 128:], v[:, :128])


def from_next(v, axis, by):
    n = lax.axis_size(axis)
    return lax.ppermute(v, axis, [(i, (i - by) % n) for i in range(n)])


def on_device(activations, output_grads, out_factors, in_factors, basis, eigvals):
    x, zl, zh = lax.axis_index("x"), lax.axis_index("zl"), lax.axis_index("zh")
    pos = jnp.stack([x, zh, lax.axis_index("y"), lax.axis_index("c"), zl])
    ff = output_grads.shape[1]

    mix = call(
        cut_kernel, jax.ShapeDtypeStruct((X, 544, 128), BF), [in_factors, activations, basis], [VMEM] * 3, 0
    )
    mix = scatter(mix, "x")
    basis_all = lax.all_gather(mix[:, 288:].reshape(1024, 128), ("y", "c"))
    acts_all = lax.all_gather(mix[:, 32:288].reshape(1024, 128), ("y", "c"))

    f = call(spread_kernel, jax.ShapeDtypeStruct((ZL * Y * C, X * KB, 128), BF), [mix], [VMEM], 0)
    grads_partner = swap(after(output_grads, f), "x", lambda i: 3 - i)
    f = scatter(f, ("zl", "y", "c"))
    o_in = swap(after(out_factors, f), "zl", lambda i: i ^ 4)

    rot = call(
        rotate_kernel, jax.ShapeDtypeStruct((X, 128, 256), F32), [f, basis_all], [VMEM] * 2, 2 * 128 * 1024 * 1024
    )
    rx = after(scatter(rot, "x"), grads_partner)
    o = jnp.concatenate([after(out_factors, rot), o_in], axis=0)
    o_in = swap(o, "zl", lambda i: i ^ 2)
    rot = jnp.sum(rx, axis=0)
    rotated = rot + after(swap(rot, "zh", lambda i: 1 - i), o_in)
    o = jnp.concatenate([after(o, rx), o_in], axis=0)
    o_in = swap(o, "zl", lambda i: i ^ 1)
    scaled = (rotated / (eigvals + DAMP)[None, :]).astype(BF)
    scaled = gather(scaled, "x")
    pt = call(
        precond_kernel, jax.ShapeDtypeStruct((Y * C, 128, 128), BF), [scaled, basis_all], [VMEM] * 2, 2 * 128 * 1024 * 1024
    )

    r2 = scatter(pt, "zl")
    o = jnp.concatenate([after(o, scaled), o_in], axis=0)
    o_other = swap(o, "x", lambda i: i ^ 1)

    part = call(
        output_kernel,
        jax.ShapeDtypeStruct((Y * C, 2 * ZL * KB, 512), F32),
        [pos, output_grads, grads_partner, after(o, pt), o_other],
        [SMEM] + [VMEM] * 4,
        2 * 512 * 512 * ff,
        [pltpu.VMEM((512, ff), BF)],
    )
    part = part[:Y] + swap(part[Y:], "c", lambda i: 1 - i)
    r2 = after(r2, part)
    s2 = jnp.sum(r2.astype(F32), axis=0).astype(BF)
    part = part[0] + sum(from_next(part[s], "y", -s) for s in (1, 2, 3))
    precond = after(gather(s2, "zl"), part, acts_all)
    out_partner = swap(part[:, 256:], "x", lambda i: 3 - i)

    ins = call(
        input_kernel, jax.ShapeDtypeStruct((X, 256, 128), F32), [acts_all, precond], [VMEM] * 2, 2 * 128 * 1024 * 1024
    )
    keep, send = call(
        sides_kernel,
        [jax.ShapeDtypeStruct((2, 128, 128), F32)] * 2,
        [pos, scatter(ins, "x"), part[:, :256], out_partner],
        [SMEM] + [VMEM] * 3,
        128 * 1024,
    )
    sides = keep + swap(send, "zh", lambda i: 1 - i)
    shares = jnp.sum((sides[0] * sides[1]).reshape(ZL * X, KB, 128), axis=1)
    pieces = shares.reshape(ZL, X, Y * C, 16).transpose(2, 3, 1, 0).reshape(Y * C, 16 * X * ZL)
    return jnp.sum(scatter(pieces, ("y", "c")), axis=0).reshape(16, X * ZL)


def solution(mesh):
    fine = Mesh(mesh.devices.reshape(X, ZL, ZH, Y, C), ("x", "zl", "zh", "y", "c"))
    dp, feats = ("x", "zl"), ("zh", "y", "c")
    return jax.shard_map(
        on_device,
        mesh=fine,
        in_specs=(P(dp, feats), P(dp, feats), P(dp, feats), P(dp, feats), P(feats, dp), P(dp)),
        out_specs=P(dp + feats, None),
        check_vma=False,
    )
```

```python
import jax
import jax.numpy as jnp
from jax import lax
from jax.experimental import pallas as pl
from jax.experimental.pallas import tpu as pltpu
from jax.sharding import Mesh, PartitionSpec as P

RANK = 32
DAMP = 0.01

X, ZL, ZH, Y, C = 4, 8, 2, 4, 2
BF = jnp.bfloat16
F32 = jnp.float32
KB = RANK // (Y * C)
XOR_ORDER = (0, 4, 2, 6, 1, 5, 3, 7)
VMEM = pl.BlockSpec(memory_space=pltpu.VMEM)
SMEM = pl.BlockSpec(memory_space=pltpu.SMEM)


def swap(v, axis, partner):
    return lax.ppermute(v, axis, [(i, partner(i)) for i in range(lax.axis_size(axis))])


def scatter(v, axis):
    return lax.all_to_all(v, axis, 0, 0, tiled=True)


def gather(v, axis):
    return scatter(jnp.broadcast_to(v[None], (lax.axis_size(axis),) + v.shape), axis)


def after(v, *others):
    return lax.optimization_barrier((v,) + others)[0]


def call(kernel, out, args, specs, flops, scratch=(), limit=24):
    many = isinstance(out, list)
    moved = sum(a.size * a.dtype.itemsize for a in args)
    return pl.pallas_call(
        kernel,
        out_shape=out,
        in_specs=specs,
        out_specs=[VMEM] * len(out) if many else VMEM,
        scratch_shapes=scratch,
        compiler_params=pltpu.CompilerParams(vmem_limit_bytes=limit * 2**20),
        cost_estimate=pl.CostEstimate(flops=flops, bytes_accessed=moved, transcendentals=0),
    )(*args)


def cut_kernel(factors, acts, basis, mix):
    for i in range(X):
        q = slice(i * 128, (i + 1) * 128)
        mix[i, :32, :] = factors[:, q]
        mix[i, 32:288, :] = acts[:, q]
        for h in range(2):
            mix[i, 288 + h * 128:416 + h * 128, :] = basis[q, h * 128:(h + 1) * 128]


def spread_kernel(mix, out):
    rows = [mix[i, :32, :].astype(F32) for i in range(X)]
    for b in range(Y * C):
        piece = jnp.concatenate([v[b * KB:(b + 1) * KB, :] for v in rows], axis=0).astype(BF)
        for zl in range(ZL):
            out[zl * Y * C + b] = piece


def rotate_kernel(f, basis, rot):
    rows = jnp.concatenate(
        [jnp.concatenate([f[zl * Y * C + s] for zl in range(ZL)], axis=0) for s in range(Y * C)], axis=1
    )
    for i in range(X):
        for h in range(2):
            at = (i * 2 + h) * 128
            b = jnp.concatenate([basis[s, at:at + 128, :] for s in range(Y * C)], axis=0)
            rot[i, :, h * 128:(h + 1) * 128] = jnp.dot(rows, b, preferred_element_type=F32)


def precond_kernel(scaled, basis, pt):
    eigs = jnp.concatenate([scaled[i] for i in range(X)], axis=1)
    for s in range(Y * C):
        b = jnp.concatenate([basis[s, j * 128:(j + 1) * 128, :] for j in range(2 * X)], axis=1)
        pt[s] = lax.dot_general(b, eigs, (((1,), (1,)), ((), ())), preferred_element_type=F32).astype(BF)


def input_kernel(acts, pt, ins):
    p = jnp.concatenate([pt[s] for s in range(Y * C)], axis=0)
    for i in range(X):
        a = jnp.concatenate([acts[s, i * 256:(i + 1) * 256, :] for s in range(Y * C)], axis=1)
        ins[i] = jnp.dot(a, p, preferred_element_type=F32)


def output_kernel(pos, g0, g1, o0, o1, part, rows):
    for dx, held in enumerate((o0, o1)):
        low = jnp.bitwise_and(jnp.bitwise_xor(pos[0], dx), 1)
        for slot, j in enumerate(XOR_ORDER):
            dst = (jnp.bitwise_xor(pos[4], j) * 2 + low) * RANK
            rows[pl.ds(pl.multiple_of(dst, RANK), RANK), :] = held[slot * RANK:(slot + 1) * RANK, :]
    for i, g in enumerate((g0, g1)):
        both = lax.dot_general(rows[...], g[...], (((1,), (1,)), ((), ())), preferred_element_type=F32)
        for b in range(Y * C):
            dc = jnp.bitwise_xor(pos[3], b % C)
            dy = lax.rem(b // C - pos[2] + Y, Y)
            for q in range(2 * ZL):
                src = q * RANK + b * KB
                part[dc * Y + dy, q * KB:(q + 1) * KB, i * 256:(i + 1) * 256] = both[src:src + KB, :]


def sides_kernel(pos, parts, out_own, out_partner, keep, send):
    ins = (parts[0] + parts[1] + parts[2] + parts[3]).T
    a, b = out_own[...], out_partner[...]
    low_x = pos[0] < 2
    low, high = jnp.where(low_x, a, b), jnp.where(low_x, b, a)
    n = 2 * KB
    outs = jnp.concatenate(
        [v[zl * n:(zl + 1) * n, :] for zl in range(ZL) for v in (low, high)], axis=0
    )
    first = pos[1] == 0
    for i, v in enumerate((ins, outs)):
        keep[i] = jnp.where(first, v[:, :128], v[:, 128:])
        send[i] = jnp.where(first, v[:, 128:], v[:, :128])


def from_next(v, axis, by):
    n = lax.axis_size(axis)
    return lax.ppermute(v, axis, [(i, (i - by) % n) for i in range(n)])


def on_device(activations, output_grads, out_factors, in_factors, basis, eigvals):
    x, zl, zh = lax.axis_index("x"), lax.axis_index("zl"), lax.axis_index("zh")
    pos = jnp.stack([x, zh, lax.axis_index("y"), lax.axis_index("c"), zl])
    ff = output_grads.shape[1]

    mix = call(
        cut_kernel, jax.ShapeDtypeStruct((X, 544, 128), BF), [in_factors, activations, basis], [VMEM] * 3, 0
    )
    mix = scatter(mix, "x")
    basis_all = lax.all_gather(mix[:, 288:].reshape(1024, 128), ("y", "c"))
    acts_all = lax.all_gather(mix[:, 32:288].reshape(1024, 128), ("y", "c"))

    f = call(spread_kernel, jax.ShapeDtypeStruct((ZL * Y * C, X * KB, 128), BF), [mix], [VMEM], 0)
    grads_partner = swap(after(output_grads, f), "x", lambda i: 3 - i)
    f = scatter(f, ("zl", "y", "c"))
    o_in = swap(after(out_factors, f), "zl", lambda i: i ^ 4)

    rot = call(
        rotate_kernel, jax.ShapeDtypeStruct((X, 128, 256), F32), [f, basis_all], [VMEM] * 2, 2 * 128 * 1024 * 1024
    )
    rx = after(scatter(rot, "x"), grads_partner)
    o = jnp.concatenate([after(out_factors, rot), o_in], axis=0)
    o_in = swap(o, "zl", lambda i: i ^ 2)
    rot = jnp.sum(rx, axis=0)
    rotated = rot + after(swap(rot, "zh", lambda i: 1 - i), o_in)
    o = jnp.concatenate([after(o, rx), o_in], axis=0)
    o_in = swap(o, "zl", lambda i: i ^ 1)
    scaled = (rotated / (eigvals + DAMP)[None, :]).astype(BF)
    scaled = gather(scaled, "x")
    pt = call(
        precond_kernel, jax.ShapeDtypeStruct((Y * C, 128, 128), BF), [scaled, basis_all], [VMEM] * 2, 2 * 128 * 1024 * 1024
    )

    r2 = scatter(pt, "zl")
    o = jnp.concatenate([after(o, scaled), o_in], axis=0)
    o_other = swap(o, "x", lambda i: i ^ 1)

    part = call(
        output_kernel,
        jax.ShapeDtypeStruct((Y * C, 2 * ZL * KB, 512), F32),
        [pos, output_grads, grads_partner, after(o, pt), o_other],
        [SMEM] + [VMEM] * 4,
        2 * 512 * 512 * ff,
        [pltpu.VMEM((512, ff), BF)],
    )
    r2 = after(r2, part)
    part = part[:Y] + swap(part[Y:], "c", lambda i: 1 - i)
    s2 = jnp.sum(r2.astype(F32), axis=0).astype(BF)
    part = part[0] + sum(from_next(part[s], "y", -s) for s in (1, 2, 3))
    precond = after(gather(s2, "zl"), part, acts_all)
    out_partner = swap(part[:, 256:], "x", lambda i: 3 - i)

    ins = call(
        input_kernel, jax.ShapeDtypeStruct((X, 256, 128), F32), [acts_all, precond], [VMEM] * 2, 2 * 128 * 1024 * 1024
    )
    keep, send = call(
        sides_kernel,
        [jax.ShapeDtypeStruct((2, 128, 128), F32)] * 2,
        [pos, scatter(ins, "x"), part[:, :256], out_partner],
        [SMEM] + [VMEM] * 3,
        128 * 1024,
    )
    sides = keep + swap(send, "zh", lambda i: 1 - i)
    shares = jnp.sum((sides[0] * sides[1]).reshape(ZL * X, KB, 128), axis=1)
    pieces = shares.reshape(ZL, X, Y * C, 16).transpose(2, 3, 1, 0).reshape(Y * C, 16 * X * ZL)
    return jnp.sum(scatter(pieces, ("y", "c")), axis=0).reshape(16, X * ZL)


def solution(mesh):
    fine = Mesh(mesh.devices.reshape(X, ZL, ZH, Y, C), ("x", "zl", "zh", "y", "c"))
    dp, feats = ("x", "zl"), ("zh", "y", "c")
    return jax.shard_map(
        on_device,
        mesh=fine,
        in_specs=(P(dp, feats), P(dp, feats), P(dp, feats), P(dp, feats), P(feats, dp), P(dp)),
        out_specs=P(dp + feats, None),
        check_vma=False,
    )
```
